128 devices in a mesh: fsdp: 32 (over y_lo, z, x), rep: 4 (over y_hi, core).
Axes of the slice: x: 4, y: 4 (y_hi: 2, y_lo: 2; y = y_hi * 2 + y_lo), z: 4, core: 2. Of those that a mesh axis runs over, the one named last changes fastest.
Arguments:
- weights: bfloat16 [16384, 32768], P(('fsdp', 'rep')), may hold values from -0.046875 to 0.046875
- exponents: int32 [128, 256], P(None, ('fsdp', 'rep')), may hold values from -10 to -5
Outputs:
- quantized: bfloat16 [16384, 32768], P(None, ('fsdp', 'rep'))
- peak: float32 [], replicated
The draws below stay inside these ranges and needn't reach their ends.
All inputs are finite; a program needn't handle non-finite values.
Results may differ from the reference program's by a relative error of at most 0.015.
Values may be sent and summed in bfloat16 or wider, within the bound.
No kernel may reach another device: no remote copies, remote signals or barrier semaphores. Data moves between devices by JAX's collectives and lax.ppermute only.
A program may use at most 128 MiB of HBM per device.

```python
import math
import jax
import jax.numpy as jnp
from jax import lax

D = 16384
FFW = 32768
INNER = 128
OUTER = 128
COLS_DEV = 256
N_FSDP = 32
N_REP = 4


def draw_exponents(key, part):
    key = jax.random.fold_in(key, 7)
    column = lax.iota(jnp.int32, FFW // INNER)
    stepped = column * 5 // (FFW // INNER)
    jitter = jax.random.randint(key, (OUTER, FFW // INNER), 0, 2)
    return (-5 - stepped[None, :] - jitter).astype(jnp.int32)


def block_levels(stream_key, extent, cuts, low, top_value):
    loudness = 1.0
    for axis_at, shards_of in cuts:
        draws = jax.random.uniform(jax.random.fold_in(jax.random.fold_in(stream_key, 6), axis_at), (shards_of,), jnp.float32, low / len(cuts), top_value / len(cuts))
        loudness = loudness * jnp.repeat(jnp.exp(draws), extent[axis_at] // shards_of).reshape((-1,) + (1,) * (len(extent) - 1 - axis_at))
    return loudness


def gaussian(own_key, dims, scale, limit, pieces=(), kind=jnp.bfloat16):
    factor_of = block_levels(own_key, dims, pieces, -0.22, 0.18) if pieces else 1.0
    array = jax.random.normal(own_key, dims, jnp.float32) * scale * factor_of
    return jnp.minimum(jnp.maximum(array, -limit), limit).astype(kind)


def setup_inputs(seed: int = 0) -> dict:
    keys = jax.random.split(jax.random.key(seed), 3)
    return {
        "weights": gaussian(keys[0], (D, FFW), D ** -0.5, 0.046875, ((0, 128),)),
        "exponents": draw_exponents(jax.random.fold_in(keys[2], 71), 0),
    }


low_power = -10
high_power = -5

def hadamard(length):
    indices = lax.iota(jnp.int32, length)
    anded = jnp.bitwise_and(indices[:, None], indices[None, :])
    parity = jnp.zeros((length, length), jnp.int32)
    for bit_place in range(length.bit_length()):
        parity = parity + anded // 2 ** bit_place % 2
    return (1 - 2 * (parity % 2)).astype(jnp.bfloat16)

def block_factor(exponents):
    factor = jnp.zeros(exponents.shape, jnp.float32)
    for exponent in range(low_power, high_power + 1):
        factor = jnp.where(exponents == exponent, jnp.float32(2.0 ** (-exponent)), factor)
    return factor

def reference(weights, exponents):
    inner_table = hadamard(INNER).astype(jnp.float32)
    outer_table = hadamard(OUTER).astype(jnp.float32)
    inner_norm = 1.0 / math.sqrt(INNER)
    outer_norm = 1.0 / math.sqrt(OUTER)
    factor = jnp.repeat(block_factor(exponents), INNER, axis=1)

    def one_strip(offset):
        columns = lax.dynamic_slice_in_dim(weights, offset, COLS_DEV, 1).astype(jnp.float32)
        columns = columns.reshape(OUTER, INNER, COLS_DEV)
        mixture = jnp.einsum('ij,ajc->aic', inner_table, columns, precision=lax.Precision.HIGHEST) * inner_norm
        mixture = lax.optimization_barrier(mixture.astype(jnp.bfloat16)).astype(jnp.float32)
        rotated = jnp.einsum('pa,aic->pic', outer_table, mixture, precision=lax.Precision.HIGHEST) * outer_norm
        scaling = lax.dynamic_slice_in_dim(factor, offset, COLS_DEV, 1)[:, None, :]
        return (rotated * scaling).astype(jnp.bfloat16).reshape(D, COLS_DEV)
    starts = jnp.arange(N_FSDP * N_REP, dtype=jnp.int32) * COLS_DEV
    stacked = lax.map(one_strip, starts)
    quantized = jnp.transpose(stacked, (1, 0, 2)).reshape(D, FFW)
    peak = jnp.max(jnp.abs(quantized.astype(jnp.float32)))
    return (quantized, peak)
```

```python
import functools

import jax
import jax.numpy as jnp
from jax import lax
from jax.experimental import pallas as pl
from jax.experimental.pallas import tpu as pltpu
from jax.sharding import PartitionSpec as P

INNER = 128
OUTER = 128
HIGH = 8
LOW = 16

low_power = -10
high_power = -5

VMEM_BYTES = 48 * 1024 * 1024


def hadamard(length):
    indices = lax.iota(jnp.int32, length)
    anded = jnp.bitwise_and(indices[:, None], indices[None, :])
    parity = jnp.zeros((length, length), jnp.int32)
    for bit_place in range(length.bit_length()):
        parity = parity + anded // 2**bit_place % 2
    return (1 - 2 * (parity % 2)).astype(jnp.bfloat16)


def block_factor(exponents):
    factor = jnp.zeros(exponents.shape, jnp.float32)
    for exponent in range(low_power, high_power + 1):
        factor = jnp.where(exponents == exponent, jnp.float32(2.0 ** (-exponent)), factor)
    return factor


def butterfly(parts):
    parts = list(parts)
    step = 1
    while step < len(parts):
        for start in range(0, len(parts), 2 * step):
            for at in range(start, start + step):
                first, second = parts[at], parts[at + step]
                parts[at], parts[at + step] = first + second, first - second
        step *= 2
    return parts


def before_kernel(weights_ref, out_ref):
    blocks, _, cols = out_ref.shape
    for block in range(blocks):
        lanes = slice(block * cols, (block + 1) * cols)
        rows = [weights_ref[LOW * k : LOW * (k + 1), lanes].astype(jnp.float32) for k in range(HIGH)]
        for k, row in enumerate(butterfly(rows)):
            out_ref[block, LOW * k : LOW * (k + 1), :] = row.astype(jnp.bfloat16)


def before(weights, devices, blocks=16):
    rows, total = weights.shape
    cols = total // devices
    return pl.pallas_call(
        before_kernel,
        out_shape=jax.ShapeDtypeStruct((devices, rows, cols), jnp.bfloat16),
        grid=(devices // blocks,),
        in_specs=[pl.BlockSpec((rows, blocks * cols), lambda n: (0, n))],
        out_specs=pl.BlockSpec((blocks, rows, cols), lambda n: (n, 0, 0)),
        compiler_params=pltpu.CompilerParams(vmem_limit_bytes=VMEM_BYTES),
        cost_estimate=pl.CostEstimate(flops=3 * rows * total, bytes_accessed=4 * rows * total, transcendentals=0),
    )(weights)


def after_kernel(table_ref, factor_ref, received_ref, out_ref, peak_ref, middle_ref):
    cols = received_ref.shape[-1]
    table = table_ref[...]
    for h in range(HIGH):
        block = received_ref[LOW * h : LOW * (h + 1)].reshape(LOW * LOW, cols)
        middle_ref[h] = jnp.dot(table, block, preferred_element_type=jnp.float32)
    largest = jnp.zeros((LOW, cols), jnp.float32)
    for low in range(LOW):
        rows = [middle_ref[h, LOW * low : LOW * (low + 1), :] for h in range(HIGH)]
        for h, row in enumerate(butterfly(rows)):
            p = h * LOW + low
            row = row * factor_ref[p : p + 1, :]
            largest = jnp.maximum(largest, jnp.abs(row))
            out_ref[p] = row.astype(jnp.bfloat16)

    @pl.when(pl.program_id(0) == 0)
    def _():
        peak_ref[...] = jnp.zeros_like(peak_ref)

    peak_ref[...] = jnp.maximum(peak_ref[...], largest)


def after(table, factor, received):
    outer, inner, cols = received.shape
    return pl.pallas_call(
        after_kernel,
        out_shape=(
            jax.ShapeDtypeStruct((outer, inner, cols), jnp.bfloat16),
            jax.ShapeDtypeStruct((LOW, cols), jnp.float32),
        ),
        grid=(inner // LOW,),
        in_specs=[
            pl.BlockSpec(table.shape, lambda n: (0, 0)),
            pl.BlockSpec(factor.shape, lambda n: (0, 0)),
            pl.BlockSpec((outer, LOW, cols), lambda n: (0, n, 0)),
        ],
        out_specs=(
            pl.BlockSpec((outer, LOW, cols), lambda n: (0, n, 0)),
            pl.BlockSpec((LOW, cols), lambda n: (0, 0)),
        ),
        scratch_shapes=[pltpu.VMEM((HIGH, LOW * LOW, cols), jnp.float32)],
        compiler_params=pltpu.CompilerParams(vmem_limit_bytes=VMEM_BYTES),
        cost_estimate=pl.CostEstimate(
            flops=2 * outer * inner * cols * LOW * LOW, bytes_accessed=4 * outer * inner * cols, transcendentals=0
        ),
    )(table, factor, received)


def on_device(weights, exponents):
    axes = ("fsdp", "rep")
    devices = lax.axis_size("fsdp") * lax.axis_size("rep")
    cols = weights.shape[1] // devices
    table = hadamard(LOW * LOW)
    factor = jnp.repeat(block_factor(exponents) * jnp.float32(1.0 / INNER), INNER, axis=1)
    packed = before(weights, devices)
    received = lax.all_to_all(packed, axes, split_axis=0, concat_axis=0, tiled=True)
    quantized, peaks = after(table, factor, received)
    peak = jnp.max(peaks).astype(jnp.bfloat16).astype(jnp.float32)
    shared = lax.all_to_all(jnp.full((devices, 1, 128), peak), axes, split_axis=0, concat_axis=0, tiled=True)
    return (quantized.reshape(OUTER * INNER, cols), jnp.max(shared))


def solution(mesh):
    return jax.shard_map(
        on_device,
        mesh=mesh,
        in_specs=(P(("fsdp", "rep"), None), P(None, ("fsdp", "rep"))),
        out_specs=(P(None, ("fsdp", "rep")), P()),
        check_vma=False,
    )
```

```python
import functools

import jax
import jax.numpy as jnp
from jax import lax
from jax.experimental import pallas as pl
from jax.experimental.pallas import tpu as pltpu
from jax.sharding import PartitionSpec as P

INNER = 128
OUTER = 128
HIGH = 8
LOW = 16

low_power = -10
high_power = -5

PIECES = 8

VMEM_BYTES = 20 * 1024 * 1024


def sylvester(length):
    bits = lax.broadcasted_iota(jnp.int32, (length, length), 0) & lax.broadcasted_iota(jnp.int32, (length, length), 1)
    for shift in (4, 2, 1):
        bits = bits ^ (bits >> shift)
    return (1 - 2 * (bits & 1)).astype(jnp.float32).astype(jnp.bfloat16)


def block_factor(exponents):
    factor = jnp.zeros(exponents.shape, jnp.float32)
    for exponent in range(low_power, high_power + 1):
        factor = jnp.where(exponents == exponent, jnp.float32(2.0 ** (-exponent)), factor)
    return factor


def butterfly(parts):
    parts = list(parts)
    step = 1
    while step < len(parts):
        for start in range(0, len(parts), 2 * step):
            for at in range(start, start + step):
                first, second = parts[at], parts[at + step]
                parts[at], parts[at + step] = first + second, first - second
        step *= 2
    return parts


def before_kernel(weights_ref, out_ref, held_ref, arrived):
    devices, _, cols = out_ref.shape
    pieces = arrived.shape[0]
    blocks = devices // pieces

    def fetch(piece):
        lanes = pl.ds(pl.multiple_of(piece * blocks * cols, blocks * cols), blocks * cols)
        return pltpu.make_async_copy(weights_ref.at[:, lanes], held_ref.at[:, lanes], arrived.at[piece])

    for piece in range(pieces):
        fetch(piece).start()

    def work(piece, carry):
        fetch(piece).wait()
        for at in range(blocks):
            block = piece * blocks + at
            lanes = pl.ds(pl.multiple_of(block * cols, cols), cols)
            rows = [held_ref[LOW * k : LOW * (k + 1), lanes].astype(jnp.float32) for k in range(HIGH)]
            for k, row in enumerate(butterfly(rows)):
                out_ref[block, LOW * k : LOW * (k + 1), :] = row.astype(jnp.bfloat16)
        return carry

    lax.fori_loop(0, pieces, work, 0)


def before(weights, devices):
    rows, total = weights.shape
    return pl.pallas_call(
        before_kernel,
        out_shape=pltpu.VMEM((devices, rows, total // devices), jnp.bfloat16),
        in_specs=[pl.BlockSpec(memory_space=pl.ANY)],
        out_specs=pl.BlockSpec(memory_space=pltpu.VMEM),
        scratch_shapes=[pltpu.VMEM(weights.shape, jnp.bfloat16), pltpu.SemaphoreType.DMA((PIECES,))],
        compiler_params=pltpu.CompilerParams(vmem_limit_bytes=VMEM_BYTES),
    )(pltpu.with_memory_space_constraint(weights, pltpu.HBM))


def after_kernel(exponents_ref, received_ref, out_ref, peak_ref, factor_ref, stage_ref, even_ref, odd_ref, written):
    cols = received_ref.shape[-1]
    groups = INNER // LOW
    table = sylvester(LOW * LOW)
    scale = block_factor(exponents_ref[...]) * jnp.float32(1.0 / INNER)
    for half in range(scale.shape[0]):
        spread = jnp.broadcast_to(scale[half : half + 1, :], (INNER, OUTER))
        factor_ref[:, half * INNER : (half + 1) * INNER] = jnp.transpose(spread)

    def rows_of(group):
        return pl.ds(pl.multiple_of(group * LOW, LOW), LOW)

    def write(group):
        return pltpu.make_async_copy(stage_ref.at[group], out_ref.at[:, rows_of(group), :], written.at[group])

    def multiply(group, middle_ref):
        for h in range(HIGH):
            block = received_ref[LOW * h : LOW * (h + 1), rows_of(group), :].reshape(LOW * LOW, cols)
            middle_ref[h] = jnp.dot(table, block, preferred_element_type=jnp.float32)

    def finish(group, middle_ref, largest):
        for low in range(LOW):
            parts = [middle_ref[h, LOW * low : LOW * (low + 1), :] for h in range(HIGH)]
            for h, part in enumerate(butterfly(parts)):
                p = h * LOW + low
                part = (part * factor_ref[p : p + 1, :]).astype(jnp.bfloat16)
                largest = jnp.maximum(largest, jnp.abs(part))
                stage_ref[group, p] = part
        write(group).start()
        return largest

    multiply(0, even_ref)

    def pair(at, largest):
        multiply(2 * at + 1, odd_ref)
        largest = finish(2 * at, even_ref, largest)
        multiply(lax.rem(2 * at + 2, groups), even_ref)
        return finish(2 * at + 1, odd_ref, largest)

    largest = lax.fori_loop(0, groups // 2, pair, jnp.zeros((LOW, cols), jnp.bfloat16))
    peak = jnp.max(largest.astype(jnp.float32), axis=(0, 1), keepdims=True)
    peak_ref[...] = jnp.broadcast_to(peak.reshape(1, 1, 1), peak_ref.shape)
    for group in range(groups):
        write(group).wait()


def after(exponents, received, devices):
    outer, inner, cols = received.shape
    groups = inner // LOW
    return pl.pallas_call(
        after_kernel,
        out_shape=(
            jax.ShapeDtypeStruct((outer, inner, cols), jnp.bfloat16),
            pltpu.VMEM((devices, 1, 128), jnp.float32),
        ),
        in_specs=[pl.BlockSpec(memory_space=pltpu.VMEM)] * 2,
        out_specs=(pl.BlockSpec(memory_space=pl.ANY), pl.BlockSpec(memory_space=pltpu.VMEM)),
        scratch_shapes=[
            pltpu.VMEM((outer, cols), jnp.float32),
            pltpu.VMEM((groups, outer, LOW, cols), jnp.bfloat16),
            pltpu.VMEM((HIGH, LOW * LOW, cols), jnp.float32),
            pltpu.VMEM((HIGH, LOW * LOW, cols), jnp.float32),
            pltpu.SemaphoreType.DMA((groups,)),
        ],
        compiler_params=pltpu.CompilerParams(vmem_limit_bytes=VMEM_BYTES),
    )(exponents, pltpu.with_memory_space_constraint(received, pltpu.VMEM))


def on_device(weights, exponents):
    axes = ("fsdp", "rep")
    devices = lax.axis_size("fsdp") * lax.axis_size("rep")
    cols = weights.shape[1] // devices
    packed = before(weights, devices)
    received = lax.all_to_all(packed, axes, split_axis=0, concat_axis=0, tiled=True)
    quantized, peaks = after(exponents.T, received, devices)
    shared = lax.all_to_all(peaks, axes, split_axis=0, concat_axis=0, tiled=True)
    return (quantized.reshape(OUTER * INNER, cols), jnp.max(shared))


def solution(mesh):
    return jax.shard_map(
        on_device,
        mesh=mesh,
        in_specs=(P(("fsdp", "rep"), None), P(None, ("fsdp", "rep"))),
        out_specs=(P(None, ("fsdp", "rep")), P()),
        check_vma=False,
    )
```

```python
import functools

import jax
import jax.numpy as jnp
from jax import lax
from jax.experimental import pallas as pl
from jax.experimental.pallas import tpu as pltpu
from jax.sharding import PartitionSpec as P

INNER = 128
OUTER = 128
HIGH = 8
LOW = 16

low_power = -10
high_power = -5

PIECES = 8
EXCHANGE_BITS = (5, 4, 0, 1, 6, 3, 2)

VMEM_BYTES = 20 * 1024 * 1024


def sylvester(length):
    bits = lax.broadcasted_iota(jnp.int32, (length, length), 0) & lax.broadcasted_iota(jnp.int32, (length, length), 1)
    for shift in (4, 2, 1):
        bits = bits ^ (bits >> shift)
    return (1 - 2 * (bits & 1)).astype(jnp.float32).astype(jnp.bfloat16)


def device_at(position):
    last = len(EXCHANGE_BITS) - 1
    return sum(((position >> (last - at)) & 1) << bit for at, bit in enumerate(EXCHANGE_BITS))


def position_of(device):
    last = len(EXCHANGE_BITS) - 1
    return sum(((device >> bit) & 1) << (last - at) for at, bit in enumerate(EXCHANGE_BITS))


def block_factor(exponents):
    factor = jnp.zeros(exponents.shape, jnp.float32)
    for exponent in range(low_power, high_power + 1):
        factor = jnp.where(exponents == exponent, jnp.float32(2.0 ** (-exponent)), factor)
    return factor


def butterfly(parts):
    parts = list(parts)
    step = 1
    while step < len(parts):
        for start in range(0, len(parts), 2 * step):
            for at in range(start, start + step):
                first, second = parts[at], parts[at + step]
                parts[at], parts[at + step] = first + second, first - second
        step *= 2
    return parts


def before_kernel(weights_ref, out_ref, held_ref, arrived):
    devices, _, cols = out_ref.shape
    pieces = arrived.shape[0]
    blocks = devices // pieces

    def fetch(piece):
        lanes = pl.ds(pl.multiple_of(piece * blocks * cols, blocks * cols), blocks * cols)
        return pltpu.make_async_copy(weights_ref.at[:, lanes], held_ref.at[:, lanes], arrived.at[piece])

    for piece in range(pieces):
        fetch(piece).start()

    def work(piece, carry):
        fetch(piece).wait()
        first = position_of(piece * blocks)
        for at in range(blocks):
            block = first + position_of(at)
            lanes = pl.ds(pl.multiple_of((piece * blocks + at) * cols, cols), cols)
            rows = [held_ref[LOW * k : LOW * (k + 1), lanes].astype(jnp.float32) for k in range(HIGH)]
            for k, row in enumerate(butterfly(rows)):
                out_ref[block, LOW * k : LOW * (k + 1), :] = row.astype(jnp.bfloat16)
        return carry

    lax.fori_loop(0, pieces, work, 0)


def before(weights, devices):
    rows, total = weights.shape
    return pl.pallas_call(
        before_kernel,
        out_shape=pltpu.VMEM((devices, rows, total // devices), jnp.bfloat16),
        in_specs=[pl.BlockSpec(memory_space=pl.ANY)],
        out_specs=pl.BlockSpec(memory_space=pltpu.VMEM),
        scratch_shapes=[pltpu.VMEM(weights.shape, jnp.bfloat16), pltpu.SemaphoreType.DMA((PIECES,))],
        compiler_params=pltpu.CompilerParams(vmem_limit_bytes=VMEM_BYTES),
    )(pltpu.with_memory_space_constraint(weights, pltpu.HBM))


def after_kernel(exponents_ref, received_ref, out_ref, peak_ref, factor_ref, stage_ref, even_ref, odd_ref, written):
    cols = received_ref.shape[-1]
    groups = INNER // LOW
    table = sylvester(LOW * LOW)
    scale = block_factor(exponents_ref[...]) * jnp.float32(1.0 / INNER)
    for half in range(scale.shape[0]):
        spread = jnp.broadcast_to(scale[half : half + 1, :], (INNER, OUTER))
        factor_ref[:, half * INNER : (half + 1) * INNER] = jnp.transpose(spread)

    def rows_of(group):
        return pl.ds(pl.multiple_of(group * LOW, LOW), LOW)

    def write(group):
        return pltpu.make_async_copy(stage_ref.at[group], out_ref.at[:, rows_of(group), :], written.at[group])

    def multiply(group, h, middle_ref):
        block = received_ref[LOW * h : LOW * (h + 1), rows_of(group), :].reshape(LOW * LOW, cols)
        middle_ref[h] = jnp.dot(table, block, preferred_element_type=jnp.float32)

    def step(group, middle_ref, following, following_ref, largest):
        for low in range(LOW):
            if low % 2 == 0:
                multiply(following, low // 2, following_ref)
            parts = [middle_ref[h, LOW * low : LOW * (low + 1), :] for h in range(HIGH)]
            for h, part in enumerate(butterfly(parts)):
                p = device_at(h * LOW + low)
                part = (part * factor_ref[p : p + 1, :]).astype(jnp.bfloat16)
                largest = jnp.maximum(largest, jnp.abs(part))
                stage_ref[group, p] = part
        write(group).start()
        return largest

    for h in range(HIGH):
        multiply(0, h, even_ref)

    def pair(at, largest):
        largest = step(2 * at, even_ref, 2 * at + 1, odd_ref, largest)
        return step(2 * at + 1, odd_ref, lax.rem(2 * at + 2, groups), even_ref, largest)

    largest = lax.fori_loop(0, groups // 2, pair, jnp.zeros((LOW, cols), jnp.bfloat16))
    peak = jnp.max(largest.astype(jnp.float32), axis=(0, 1), keepdims=True)
    peak_ref[...] = jnp.broadcast_to(peak.reshape(1, 1, 1), peak_ref.shape)
    for group in range(groups):
        write(group).wait()


def after(exponents, received, devices):
    outer, inner, cols = received.shape
    groups = inner // LOW
    return pl.pallas_call(
        after_kernel,
        out_shape=(
            jax.ShapeDtypeStruct((outer, inner, cols), jnp.bfloat16),
            pltpu.VMEM((devices, 1, 128), jnp.float32),
        ),
        in_specs=[pl.BlockSpec(memory_space=pltpu.VMEM)] * 2,
        out_specs=(pl.BlockSpec(memory_space=pl.ANY), pl.BlockSpec(memory_space=pltpu.VMEM)),
        scratch_shapes=[
            pltpu.VMEM((outer, cols), jnp.float32),
            pltpu.VMEM((groups, outer, LOW, cols), jnp.bfloat16),
            pltpu.VMEM((HIGH, LOW * LOW, cols), jnp.float32),
            pltpu.VMEM((HIGH, LOW * LOW, cols), jnp.float32),
            pltpu.SemaphoreType.DMA((groups,)),
        ],
        compiler_params=pltpu.CompilerParams(vmem_limit_bytes=VMEM_BYTES),
    )(exponents, pltpu.with_memory_space_constraint(received, pltpu.VMEM))


def on_device(weights, exponents):
    axes = ("fsdp", "rep")
    devices = lax.axis_size("fsdp") * lax.axis_size("rep")
    cols = weights.shape[1] // devices
    packed = before(weights, devices)
    order = [[device_at(position) for position in range(devices)]]
    exchange = functools.partial(
        lax.all_to_all, axis_name=axes, split_axis=0, concat_axis=0, axis_index_groups=order, tiled=True
    )
    received = exchange(packed)
    quantized, peaks = after(exponents.T, received, devices)
    shared = exchange(peaks)
    return (quantized.reshape(OUTER * INNER, cols), jnp.max(shared))


def solution(mesh):
    return jax.shard_map(
        on_device,
        mesh=mesh,
        in_specs=(P(("fsdp", "rep"), None), P(None, ("fsdp", "rep"))),
        out_specs=(P(None, ("fsdp", "rep")), P()),
        check_vma=False,
    )
```

```python
import functools

import jax
import jax.numpy as jnp
from jax import lax
from jax.experimental import pallas as pl
from jax.experimental.pallas import tpu as pltpu
from jax.sharding import PartitionSpec as P

INNER = 128
OUTER = 128
HIGH = 8
LOW = 16

low_power = -10
high_power = -5

PIECES = 8
EXCHANGE_BITS = (5, 4, 0, 1, 6, 3, 2)

VMEM_BYTES = 20 * 1024 * 1024


def sylvester(length):
    bits = lax.broadcasted_iota(jnp.int32, (length, length), 0) & lax.broadcasted_iota(jnp.int32, (length, length), 1)
    for shift in (4, 2, 1):
        bits = bits ^ (bits >> shift)
    return (1 - 2 * (bits & 1)).astype(jnp.float32).astype(jnp.bfloat16)


def device_at(position):
    last = len(EXCHANGE_BITS) - 1
    return sum(((position >> (last - at)) & 1) << bit for at, bit in enumerate(EXCHANGE_BITS))


def position_of(device):
    last = len(EXCHANGE_BITS) - 1
    return sum(((device >> bit) & 1) << (last - at) for at, bit in enumerate(EXCHANGE_BITS))


def block_factor(exponents):
    factor = jnp.zeros(exponents.shape, jnp.float32)
    for exponent in range(low_power, high_power + 1):
        factor = jnp.where(exponents == exponent, jnp.float32(2.0 ** (-exponent)), factor)
    return factor


def butterfly(parts):
    parts = list(parts)
    step = 1
    while step < len(parts):
        for start in range(0, len(parts), 2 * step):
            for at in range(start, start + step):
                first, second = parts[at], parts[at + step]
                parts[at], parts[at + step] = first + second, first - second
        step *= 2
    return parts


def before_kernel(weights_ref, out_ref, held_ref, arrived):
    devices, _, cols = out_ref.shape
    pieces = arrived.shape[0]
    blocks = devices // pieces

    def fetch(piece):
        lanes = pl.ds(pl.multiple_of(piece * blocks * cols, blocks * cols), blocks * cols)
        return pltpu.make_async_copy(weights_ref.at[:, lanes], held_ref.at[:, lanes], arrived.at[piece])

    for piece in range(pieces):
        fetch(piece).start()

    def work(piece, carry):
        fetch(piece).wait()
        first = position_of(piece * blocks)
        for at in range(blocks):
            block = first + position_of(at)
            lanes = pl.ds(pl.multiple_of((piece * blocks + at) * cols, cols), cols)
            rows = [held_ref[LOW * k : LOW * (k + 1), lanes].astype(jnp.float32) for k in range(HIGH)]
            for k, row in enumerate(butterfly(rows)):
                out_ref[block, LOW * k : LOW * (k + 1), :] = row.astype(jnp.bfloat16)
        return carry

    lax.fori_loop(0, pieces, work, 0)


def before(weights, devices):
    rows, total = weights.shape
    return pl.pallas_call(
        before_kernel,
        out_shape=pltpu.VMEM((devices, rows, total // devices), jnp.bfloat16),
        in_specs=[pl.BlockSpec(memory_space=pl.ANY)],
        out_specs=pl.BlockSpec(memory_space=pltpu.VMEM),
        scratch_shapes=[pltpu.VMEM(weights.shape, jnp.bfloat16), pltpu.SemaphoreType.DMA((PIECES,))],
        compiler_params=pltpu.CompilerParams(vmem_limit_bytes=VMEM_BYTES),
    )(pltpu.with_memory_space_constraint(weights, pltpu.HBM))


def after_kernel(exponents_ref, received_ref, out_ref, peak_ref, factor_ref, stage_ref, even_ref, odd_ref, written):
    cols = received_ref.shape[-1]
    groups = INNER // LOW
    table = sylvester(LOW * LOW)
    scale = block_factor(exponents_ref[...]) * jnp.float32(1.0 / INNER)
    for half in range(scale.shape[0]):
        spread = jnp.broadcast_to(scale[half : half + 1, :], (INNER, OUTER))
        factor_ref[:, half * INNER : (half + 1) * INNER] = jnp.transpose(spread)

    def rows_of(group):
        return slice(group * LOW, (group + 1) * LOW)

    def write(group):
        return pltpu.make_async_copy(stage_ref.at[group], out_ref.at[:, rows_of(group), :], written.at[group])

    def multiply(group, h, middle_ref):
        block = received_ref[LOW * h : LOW * (h + 1), rows_of(group), :].reshape(LOW * LOW, cols)
        middle_ref[h] = jnp.dot(table, block, preferred_element_type=jnp.float32)

    def step(group, middle_ref, following, following_ref, largest):
        for low in range(LOW):
            if low % 2 == 0 and following < groups:
                multiply(following, low // 2, following_ref)
            parts = [middle_ref[h, LOW * low : LOW * (low + 1), :] for h in range(HIGH)]
            for h, part in enumerate(butterfly(parts)):
                p = device_at(h * LOW + low)
                part = (part * factor_ref[p : p + 1, :]).astype(jnp.bfloat16)
                largest = jnp.maximum(largest, jnp.abs(part))
                stage_ref[group, p] = part
        write(group).start()
        return largest

    for h in range(HIGH):
        multiply(0, h, even_ref)

    largest = jnp.zeros((LOW, cols), jnp.bfloat16)
    refs = (even_ref, odd_ref)
    for group in range(groups):
        largest = step(group, refs[group % 2], group + 1, refs[(group + 1) % 2], largest)
    peak = jnp.max(largest.astype(jnp.float32), axis=(0, 1), keepdims=True)
    peak_ref[...] = jnp.broadcast_to(peak.reshape(1, 1, 1), peak_ref.shape)
    for group in range(groups):
        write(group).wait()


def after(exponents, received, devices):
    outer, inner, cols = received.shape
    groups = inner // LOW
    return pl.pallas_call(
        after_kernel,
        out_shape=(
            jax.ShapeDtypeStruct((outer, inner, cols), jnp.bfloat16),
            pltpu.VMEM((devices, 1, 128), jnp.float32),
        ),
        in_specs=[pl.BlockSpec(memory_space=pltpu.VMEM)] * 2,
        out_specs=(pl.BlockSpec(memory_space=pl.ANY), pl.BlockSpec(memory_space=pltpu.VMEM)),
        scratch_shapes=[
            pltpu.VMEM((outer, cols), jnp.float32),
            pltpu.VMEM((groups, outer, LOW, cols), jnp.bfloat16),
            pltpu.VMEM((HIGH, LOW * LOW, cols), jnp.float32),
            pltpu.VMEM((HIGH, LOW * LOW, cols), jnp.float32),
            pltpu.SemaphoreType.DMA((groups,)),
        ],
        compiler_params=pltpu.CompilerParams(vmem_limit_bytes=VMEM_BYTES),
    )(exponents, pltpu.with_memory_space_constraint(received, pltpu.VMEM))


def on_device(weights, exponents):
    axes = ("fsdp", "rep")
    devices = lax.axis_size("fsdp") * lax.axis_size("rep")
    cols = weights.shape[1] // devices
    packed = before(weights, devices)
    order = [[device_at(position) for position in range(devices)]]
    exchange = functools.partial(
        lax.all_to_all, axis_name=axes, split_axis=0, concat_axis=0, axis_index_groups=order, tiled=True
    )
    received = exchange(packed)
    quantized, peaks = after(exponents.T, received, devices)
    shared = exchange(peaks)
    return (quantized.reshape(OUTER * INNER, cols), jnp.max(shared))


def solution(mesh):
    return jax.shard_map(
        on_device,
        mesh=mesh,
        in_specs=(P(("fsdp", "rep"), None), P(None, ("fsdp", "rep"))),
        out_specs=(P(None, ("fsdp", "rep")), P()),
        check_vma=False,
    )
```

```python
import functools

import jax
import jax.numpy as jnp
from jax import lax
from jax.experimental import pallas as pl
from jax.experimental.pallas import tpu as pltpu
from jax.sharding import PartitionSpec as P

INNER = 128
OUTER = 128
HIGH = 8
LOW = 16

low_power = -10
high_power = -5

PIECES = 16
EXCHANGE_BITS = (5, 4, 0, 1, 6, 3, 2)

VMEM_BYTES = 20 * 1024 * 1024


def sylvester(length):
    bits = lax.broadcasted_iota(jnp.int32, (length, length), 0) & lax.broadcasted_iota(jnp.int32, (length, length), 1)
    for shift in (4, 2, 1):
        bits = bits ^ (bits >> shift)
    return (1 - 2 * (bits & 1)).astype(jnp.float32).astype(jnp.bfloat16)


def device_at(position):
    last = len(EXCHANGE_BITS) - 1
    return sum(((position >> (last - at)) & 1) << bit for at, bit in enumerate(EXCHANGE_BITS))


def position_of(device):
    last = len(EXCHANGE_BITS) - 1
    return sum(((device >> bit) & 1) << (last - at) for at, bit in enumerate(EXCHANGE_BITS))


def block_factor(exponents):
    factor = jnp.zeros(exponents.shape, jnp.float32)
    for exponent in range(low_power, high_power + 1):
        factor = jnp.where(exponents == exponent, jnp.float32(2.0 ** (-exponent)), factor)
    return factor


def butterfly(parts):
    parts = list(parts)
    step = 1
    while step < len(parts):
        for start in range(0, len(parts), 2 * step):
            for at in range(start, start + step):
                first, second = parts[at], parts[at + step]
                parts[at], parts[at + step] = first + second, first - second
        step *= 2
    return parts


def before_kernel(weights_ref, out_ref, held_ref, arrived):
    devices, _, cols = out_ref.shape
    pieces = arrived.shape[0]
    blocks = devices // pieces

    def fetch(piece):
        lanes = pl.ds(pl.multiple_of(piece * blocks * cols, blocks * cols), blocks * cols)
        return pltpu.make_async_copy(weights_ref.at[:, lanes], held_ref.at[:, lanes], arrived.at[piece])

    for piece in range(pieces):
        fetch(piece).start()

    def work(piece, carry):
        fetch(piece).wait()
        first = position_of(piece * blocks)
        for at in range(blocks):
            block = first + position_of(at)
            lanes = pl.ds(pl.multiple_of((piece * blocks + at) * cols, cols), cols)
            rows = [held_ref[LOW * k : LOW * (k + 1), lanes].astype(jnp.float32) for k in range(HIGH)]
            for k, row in enumerate(butterfly(rows)):
                out_ref[block, LOW * k : LOW * (k + 1), :] = row.astype(jnp.bfloat16)
        return carry

    lax.fori_loop(0, pieces, work, 0)


def before(weights, devices):
    rows, total = weights.shape
    return pl.pallas_call(
        before_kernel,
        out_shape=pltpu.VMEM((devices, rows, total // devices), jnp.bfloat16),
        in_specs=[pl.BlockSpec(memory_space=pl.ANY)],
        out_specs=pl.BlockSpec(memory_space=pltpu.VMEM),
        scratch_shapes=[pltpu.VMEM(weights.shape, jnp.bfloat16), pltpu.SemaphoreType.DMA((PIECES,))],
        compiler_params=pltpu.CompilerParams(vmem_limit_bytes=VMEM_BYTES),
    )(pltpu.with_memory_space_constraint(weights, pltpu.HBM))


def after_kernel(exponents_ref, received_ref, out_ref, peak_ref, factor_ref, stage_ref, even_ref, odd_ref, written):
    cols = received_ref.shape[-1]
    groups = INNER // LOW
    table = sylvester(LOW * LOW)
    scale = block_factor(exponents_ref[...]) * jnp.float32(1.0 / INNER)
    for half in range(scale.shape[0]):
        spread = jnp.broadcast_to(scale[half : half + 1, :], (INNER, OUTER))
        factor_ref[:, half * INNER : (half + 1) * INNER] = jnp.transpose(spread)

    def rows_of(group):
        return slice(group * LOW, (group + 1) * LOW)

    def write(group):
        return pltpu.make_async_copy(stage_ref.at[group], out_ref.at[:, rows_of(group), :], written.at[group])

    def prepare(group, low, middle_ref):
        parts = [received_ref[h * LOW + low, rows_of(group), :] for h in range(HIGH)]
        for h, part in enumerate(butterfly(parts)):
            middle_ref[h, LOW * low : LOW * (low + 1), :] = part.astype(jnp.bfloat16)

    refs = (even_ref, odd_ref)
    for low in range(LOW):
        prepare(0, low, even_ref)
    largest = jnp.zeros((LOW, cols), jnp.bfloat16)
    for group in range(groups):
        for h in range(HIGH):
            product = jnp.dot(table, refs[group % 2][h], preferred_element_type=jnp.float32)
            if group + 1 < groups:
                for low in (2 * h, 2 * h + 1):
                    prepare(group + 1, low, refs[(group + 1) % 2])
            for low in range(LOW):
                p = device_at(h * LOW + low)
                part = (product[LOW * low : LOW * (low + 1), :] * factor_ref[p : p + 1, :]).astype(jnp.bfloat16)
                largest = jnp.maximum(largest, jnp.abs(part))
                stage_ref[group, p] = part
        write(group).start()

    peak = jnp.max(largest.astype(jnp.float32), axis=(0, 1), keepdims=True)
    peak_ref[...] = jnp.broadcast_to(peak.reshape(1, 1, 1), peak_ref.shape)
    for group in range(groups):
        write(group).wait()


def after(exponents, received, devices):
    outer, inner, cols = received.shape
    groups = inner // LOW
    return pl.pallas_call(
        after_kernel,
        out_shape=(
            jax.ShapeDtypeStruct((outer, inner, cols), jnp.bfloat16),
            pltpu.VMEM((devices, 1, 128), jnp.float32),
        ),
        in_specs=[pl.BlockSpec(memory_space=pltpu.VMEM)] * 2,
        out_specs=(pl.BlockSpec(memory_space=pl.ANY), pl.BlockSpec(memory_space=pltpu.VMEM)),
        scratch_shapes=[
            pltpu.VMEM((outer, cols), jnp.float32),
            pltpu.VMEM((groups, outer, LOW, cols), jnp.bfloat16),
            pltpu.VMEM((HIGH, LOW * LOW, cols), jnp.bfloat16),
            pltpu.VMEM((HIGH, LOW * LOW, cols), jnp.bfloat16),
            pltpu.SemaphoreType.DMA((groups,)),
        ],
        compiler_params=pltpu.CompilerParams(vmem_limit_bytes=VMEM_BYTES),
    )(exponents, pltpu.with_memory_space_constraint(received, pltpu.VMEM))


def on_device(weights, exponents):
    axes = ("fsdp", "rep")
    devices = lax.axis_size("fsdp") * lax.axis_size("rep")
    cols = weights.shape[1] // devices
    packed = before(weights, devices)
    order = [[device_at(position) for position in range(devices)]]
    exchange = functools.partial(
        lax.all_to_all, axis_name=axes, split_axis=0, concat_axis=0, axis_index_groups=order, tiled=True
    )
    received = exchange(packed)
    quantized, peaks = after(exponents.T, received, devices)
    shared = exchange(peaks)
    return (quantized.reshape(OUTER * INNER, cols), jnp.max(shared))


def solution(mesh):
    return jax.shard_map(
        on_device,
        mesh=mesh,
        in_specs=(P(("fsdp", "rep"), None), P(None, ("fsdp", "rep"))),
        out_specs=(P(None, ("fsdp", "rep")), P()),
        check_vma=False,
    )
```

```python
import functools

import jax
import jax.numpy as jnp
from jax import lax
from jax.experimental import pallas as pl
from jax.experimental.pallas import tpu as pltpu
from jax.sharding import PartitionSpec as P

INNER = 128
OUTER = 128
HIGH = 8
LOW = 16

low_power = -10
high_power = -5

PIECES = 16
WIDE = 2
WRITTEN = 4
EXCHANGE_BITS = (5, 4, 0, 1, 6, 3, 2)

VMEM_BYTES = 20 * 1024 * 1024


def sylvester(length):
    bits = lax.broadcasted_iota(jnp.int32, (length, length), 0) & lax.broadcasted_iota(jnp.int32, (length, length), 1)
    for shift in (4, 2, 1):
        bits = bits ^ (bits >> shift)
    return (1 - 2 * (bits & 1)).astype(jnp.float32).astype(jnp.bfloat16)


def device_at(position):
    last = len(EXCHANGE_BITS) - 1
    return sum(((position >> (last - at)) & 1) << bit for at, bit in enumerate(EXCHANGE_BITS))


def position_of(device):
    last = len(EXCHANGE_BITS) - 1
    return sum(((device >> bit) & 1) << (last - at) for at, bit in enumerate(EXCHANGE_BITS))


def block_factor(exponents):
    factor = jnp.zeros(exponents.shape, jnp.float32)
    for exponent in range(low_power, high_power + 1):
        factor = jnp.where(exponents == exponent, jnp.float32(2.0 ** (-exponent)), factor)
    return factor


def butterfly(parts):
    parts = list(parts)
    step = 1
    while step < len(parts):
        for start in range(0, len(parts), 2 * step):
            for at in range(start, start + step):
                first, second = parts[at], parts[at + step]
                parts[at], parts[at + step] = first + second, first - second
        step *= 2
    return parts


def before_kernel(weights_ref, out_ref, held_ref, arrived):
    devices, _, cols = out_ref.shape
    pieces = arrived.shape[0]
    blocks = devices // pieces

    def fetch(piece):
        lanes = pl.ds(pl.multiple_of(piece * blocks * cols, blocks * cols), blocks * cols)
        return pltpu.make_async_copy(weights_ref.at[:, lanes], held_ref.at[:, lanes], arrived.at[piece])

    for piece in range(pieces):
        fetch(piece).start()

    def work(piece, carry):
        fetch(piece).wait()
        first = position_of(piece * blocks)
        for at in range(blocks):
            block = first + position_of(at)
            lanes = pl.ds(pl.multiple_of((piece * blocks + at) * cols, cols), cols)
            rows = [held_ref[LOW * k : LOW * (k + 1), lanes].astype(jnp.float32) for k in range(HIGH)]
            for k, row in enumerate(butterfly(rows)):
                out_ref[block, LOW * k : LOW * (k + 1), :] = row.astype(jnp.bfloat16)
        return carry

    lax.fori_loop(0, pieces, work, 0)


def before(weights, devices):
    rows, total = weights.shape
    return pl.pallas_call(
        before_kernel,
        out_shape=pltpu.VMEM((devices, rows, total // devices), jnp.bfloat16),
        in_specs=[pl.BlockSpec(memory_space=pl.ANY)],
        out_specs=pl.BlockSpec(memory_space=pltpu.VMEM),
        scratch_shapes=[pltpu.VMEM(weights.shape, jnp.bfloat16), pltpu.SemaphoreType.DMA((PIECES,))],
        compiler_params=pltpu.CompilerParams(vmem_limit_bytes=VMEM_BYTES),
    )(pltpu.with_memory_space_constraint(weights, pltpu.HBM))


def after_kernel(exponents_ref, received_ref, out_ref, peak_ref, factor_ref, stage_ref, even_ref, odd_ref, written):
    cols = received_ref.shape[-1]
    groups = INNER // LOW
    table = sylvester(LOW * LOW)
    scale = block_factor(exponents_ref[...]) * jnp.float32(1.0 / INNER)
    for half in range(scale.shape[0]):
        spread = jnp.broadcast_to(scale[half : half + 1, :], (INNER, OUTER))
        factor_ref[:, half * INNER : (half + 1) * INNER] = jnp.transpose(spread)

    def write(group, first):
        outer = slice(first * LOW, (first + WRITTEN) * LOW)
        rows = slice(group * LOW, (group + 1) * LOW)
        return pltpu.make_async_copy(
            stage_ref.at[group, outer], out_ref.at[outer, rows, :], written.at[group, first // WRITTEN]
        )

    def prepare(group, low, middle_ref):
        rows = slice(group * LOW, (group + 1) * LOW)
        parts = [received_ref[position_of(h * LOW + low), rows, :] for h in range(HIGH)]
        for h, part in enumerate(butterfly(parts)):
            lanes = slice(h % WIDE * cols, (h % WIDE + 1) * cols)
            middle_ref[h // WIDE, LOW * low : LOW * (low + 1), lanes] = part

    refs = (even_ref, odd_ref)
    for low in range(LOW):
        prepare(0, low, even_ref)
    largest = jnp.zeros((LOW, cols), jnp.bfloat16)
    for group in range(groups):
        for first in range(0, HIGH, WIDE):
            product = jnp.dot(table, refs[group % 2][first // WIDE], preferred_element_type=jnp.float32)
            if group + 1 < groups:
                for low in range(first * LOW // HIGH, (first + WIDE) * LOW // HIGH):
                    prepare(group + 1, low, refs[(group + 1) % 2])
            for low in range(LOW):
                for h in range(first, first + WIDE):
                    p = h * LOW + low
                    part = product[LOW * low : LOW * (low + 1), (h - first) * cols : (h - first + 1) * cols]
                    part = (part * factor_ref[p : p + 1, :]).astype(jnp.bfloat16)
                    largest = jnp.maximum(largest, jnp.abs(part))
                    stage_ref[group, p] = part
            if (first + WIDE) % WRITTEN == 0:
                write(group, first + WIDE - WRITTEN).start()

    peak = jnp.max(largest.astype(jnp.float32), axis=(0, 1), keepdims=True)
    peak_ref[...] = jnp.broadcast_to(peak.reshape(1, 1, 1), peak_ref.shape)
    for group in range(groups):
        for first in range(0, HIGH, WRITTEN):
            write(group, first).wait()


def after(exponents, received, devices):
    outer, inner, cols = received.shape
    groups = inner // LOW
    return pl.pallas_call(
        after_kernel,
        out_shape=(
            jax.ShapeDtypeStruct((outer, inner, cols), jnp.bfloat16),
            pltpu.VMEM((devices, 1, 128), jnp.float32),
        ),
        in_specs=[pl.BlockSpec(memory_space=pltpu.VMEM)] * 2,
        out_specs=(pl.BlockSpec(memory_space=pl.ANY), pl.BlockSpec(memory_space=pltpu.VMEM)),
        scratch_shapes=[
            pltpu.VMEM((outer, cols), jnp.float32),
            pltpu.VMEM((groups, outer, LOW, cols), jnp.bfloat16),
            pltpu.VMEM((HIGH // WIDE, LOW * LOW, WIDE * cols), jnp.bfloat16),
            pltpu.VMEM((HIGH // WIDE, LOW * LOW, WIDE * cols), jnp.bfloat16),
            pltpu.SemaphoreType.DMA((groups, HIGH // WRITTEN)),
        ],
        compiler_params=pltpu.CompilerParams(vmem_limit_bytes=VMEM_BYTES),
    )(exponents, pltpu.with_memory_space_constraint(received, pltpu.VMEM))


def on_device(weights, exponents):
    axes = ("fsdp", "rep")
    devices = lax.axis_size("fsdp") * lax.axis_size("rep")
    cols = weights.shape[1] // devices
    packed = before(weights, devices)
    order = [[device_at(position) for position in range(devices)]]
    exchange = functools.partial(
        lax.all_to_all, axis_name=axes, split_axis=0, concat_axis=0, axis_index_groups=order, tiled=True
    )
    received = exchange(packed)
    quantized, peaks = after(exponents.T, received, devices)
    shared = exchange(peaks)
    return (quantized.reshape(OUTER * INNER, cols), jnp.max(shared.reshape(devices, 128)[:, :1]))


def solution(mesh):
    return jax.shard_map(
        on_device,
        mesh=mesh,
        in_specs=(P(("fsdp", "rep"), None), P(None, ("fsdp", "rep"))),
        out_specs=(P(None, ("fsdp", "rep")), P()),
        check_vma=False,
    )
```

```python
import functools

import jax
import jax.numpy as jnp
from jax import lax
from jax.experimental import pallas as pl
from jax.experimental.pallas import tpu as pltpu
from jax.sharding import PartitionSpec as P

INNER = 128
OUTER = 128
HIGH = 8
LOW = 16

low_power = -10
high_power = -5

PIECES = 16
WIDE = 2
WRITTEN = 4
EXCHANGE_BITS = (5, 4, 0, 3, 2, 1, 6)

VMEM_BYTES = 20 * 1024 * 1024


def sylvester(length):
    bits = lax.broadcasted_iota(jnp.int32, (length, length), 0) & lax.broadcasted_iota(jnp.int32, (length, length), 1)
    for shift in (4, 2, 1):
        bits = bits ^ (bits >> shift)
    return (1 - 2 * (bits & 1)).astype(jnp.float32).astype(jnp.bfloat16)


def device_at(position):
    last = len(EXCHANGE_BITS) - 1
    return sum(((position >> (last - at)) & 1) << bit for at, bit in enumerate(EXCHANGE_BITS))


def position_of(device):
    last = len(EXCHANGE_BITS) - 1
    return sum(((device >> bit) & 1) << (last - at) for at, bit in enumerate(EXCHANGE_BITS))


def block_factor(exponents):
    factor = jnp.zeros(exponents.shape, jnp.float32)
    for exponent in range(low_power, high_power + 1):
        factor = jnp.where(exponents == exponent, jnp.float32(2.0 ** (-exponent)), factor)
    return factor


def butterfly(parts):
    parts = list(parts)
    step = 1
    while step < len(parts):
        for start in range(0, len(parts), 2 * step):
            for at in range(start, start + step):
                first, second = parts[at], parts[at + step]
                parts[at], parts[at + step] = first + second, first - second
        step *= 2
    return parts


def before_kernel(weights_ref, out_ref, held_ref, arrived):
    devices, _, cols = out_ref.shape
    pieces = arrived.shape[0]
    blocks = devices // pieces

    def fetch(piece):
        lanes = pl.ds(pl.multiple_of(piece * blocks * cols, blocks * cols), blocks * cols)
        return pltpu.make_async_copy(weights_ref.at[:, lanes], held_ref.at[:, lanes], arrived.at[piece])

    for piece in range(pieces):
        fetch(piece).start()

    def work(piece, carry):
        fetch(piece).wait()
        first = position_of(piece * blocks)
        for at in range(blocks):
            block = first + position_of(at)
            lanes = pl.ds(pl.multiple_of((piece * blocks + at) * cols, cols), cols)
            rows = [held_ref[LOW * k : LOW * (k + 1), lanes].astype(jnp.float32) for k in range(HIGH)]
            for k, row in enumerate(butterfly(rows)):
                out_ref[block, LOW * k : LOW * (k + 1), :] = row.astype(jnp.bfloat16)
        return carry

    lax.fori_loop(0, pieces, work, 0)


def before(weights, devices):
    rows, total = weights.shape
    return pl.pallas_call(
        before_kernel,
        out_shape=pltpu.VMEM((devices, rows, total // devices), jnp.bfloat16),
        in_specs=[pl.BlockSpec(memory_space=pl.ANY)],
        out_specs=pl.BlockSpec(memory_space=pltpu.VMEM),
        scratch_shapes=[pltpu.VMEM(weights.shape, jnp.bfloat16), pltpu.SemaphoreType.DMA((PIECES,))],
        compiler_params=pltpu.CompilerParams(vmem_limit_bytes=VMEM_BYTES),
    )(pltpu.with_memory_space_constraint(weights, pltpu.HBM))


def after_kernel(exponents_ref, received_ref, out_ref, peak_ref, factor_ref, stage_ref, even_ref, odd_ref, written):
    cols = received_ref.shape[-1]
    groups = INNER // LOW
    table = sylvester(LOW * LOW)
    scale = block_factor(exponents_ref[...]) * jnp.float32(1.0 / INNER)
    for half in range(scale.shape[0]):
        spread = jnp.broadcast_to(scale[half : half + 1, :], (INNER, OUTER))
        factor_ref[:, half * INNER : (half + 1) * INNER] = jnp.transpose(spread)

    def write(group, first):
        outer = slice(first * LOW, (first + WRITTEN) * LOW)
        rows = slice(group * LOW, (group + 1) * LOW)
        return pltpu.make_async_copy(
            stage_ref.at[group, outer], out_ref.at[outer, rows, :], written.at[group, first // WRITTEN]
        )

    def prepare(group, low, middle_ref):
        rows = slice(group * LOW, (group + 1) * LOW)
        parts = [received_ref[position_of(h * LOW + low), rows, :] for h in range(HIGH)]
        for h, part in enumerate(butterfly(parts)):
            lanes = slice(h % WIDE * cols, (h % WIDE + 1) * cols)
            middle_ref[h // WIDE, LOW * low : LOW * (low + 1), lanes] = part

    refs = (even_ref, odd_ref)
    for low in range(LOW):
        prepare(0, low, even_ref)
    largest = jnp.zeros((LOW, cols), jnp.bfloat16)
    for group in range(groups):
        for first in range(0, HIGH, WIDE):
            product = jnp.dot(table, refs[group % 2][first // WIDE], preferred_element_type=jnp.float32)
            if group + 1 < groups:
                for low in range(first * LOW // HIGH, (first + WIDE) * LOW // HIGH):
                    prepare(group + 1, low, refs[(group + 1) % 2])
            for low in range(LOW):
                for h in range(first, first + WIDE):
                    p = h * LOW + low
                    part = product[LOW * low : LOW * (low + 1), (h - first) * cols : (h - first + 1) * cols]
                    part = (part * factor_ref[p : p + 1, :]).astype(jnp.bfloat16)
                    largest = jnp.maximum(largest, jnp.abs(part))
                    stage_ref[group, p] = part
            if (first + WIDE) % WRITTEN == 0:
                write(group, first + WIDE - WRITTEN).start()

    peak = jnp.max(largest.astype(jnp.float32), axis=(0, 1), keepdims=True)
    peak_ref[...] = jnp.broadcast_to(peak.reshape(1, 1, 1), peak_ref.shape)
    for group in range(groups):
        for first in range(0, HIGH, WRITTEN):
            write(group, first).wait()


def after(exponents, received, devices):
    outer, inner, cols = received.shape
    groups = inner // LOW
    return pl.pallas_call(
        after_kernel,
        out_shape=(
            jax.ShapeDtypeStruct((outer, inner, cols), jnp.bfloat16),
            pltpu.VMEM((devices, 1, 128), jnp.float32),
        ),
        in_specs=[pl.BlockSpec(memory_space=pltpu.VMEM)] * 2,
        out_specs=(pl.BlockSpec(memory_space=pl.ANY), pl.BlockSpec(memory_space=pltpu.VMEM)),
        scratch_shapes=[
            pltpu.VMEM((outer, cols), jnp.float32),
            pltpu.VMEM((groups, outer, LOW, cols), jnp.bfloat16),
            pltpu.VMEM((HIGH // WIDE, LOW * LOW, WIDE * cols), jnp.bfloat16),
            pltpu.VMEM((HIGH // WIDE, LOW * LOW, WIDE * cols), jnp.bfloat16),
            pltpu.SemaphoreType.DMA((groups, HIGH // WRITTEN)),
        ],
        compiler_params=pltpu.CompilerParams(vmem_limit_bytes=VMEM_BYTES),
    )(exponents, pltpu.with_memory_space_constraint(received, pltpu.VMEM))


def on_device(weights, exponents):
    axes = ("fsdp", "rep")
    devices = lax.axis_size("fsdp") * lax.axis_size("rep")
    cols = weights.shape[1] // devices
    packed = before(weights, devices)
    order = [[device_at(position) for position in range(devices)]]
    exchange = functools.partial(
        lax.all_to_all, axis_name=axes, split_axis=0, concat_axis=0, axis_index_groups=order, tiled=True
    )
    received = exchange(packed)
    quantized, peaks = after(exponents.T, received, devices)
    shared = exchange(peaks)
    return (quantized.reshape(OUTER * INNER, cols), jnp.max(shared.reshape(devices, 128)[:, :1]))


def solution(mesh):
    return jax.shard_map(
        on_device,
        mesh=mesh,
        in_specs=(P(("fsdp", "rep"), None), P(None, ("fsdp", "rep"))),
        out_specs=(P(None, ("fsdp", "rep")), P()),
        check_vma=False,
    )
```

```python
import functools

import jax
import jax.numpy as jnp
from jax import lax
from jax.experimental import pallas as pl
from jax.experimental.pallas import tpu as pltpu
from jax.sharding import PartitionSpec as P

INNER = 128
OUTER = 128
HIGH = 8
LOW = 16

low_power = -10
high_power = -5

PIECES = 16
WIDE = 2
WRITTEN = 4
EXCHANGE_BITS = (1, 6, 0, 5, 4, 3, 2)

VMEM_BYTES = 20 * 1024 * 1024


def sylvester(length):
    bits = lax.broadcasted_iota(jnp.int32, (length, length), 0) & lax.broadcasted_iota(jnp.int32, (length, length), 1)
    for shift in (4, 2, 1):
        bits = bits ^ (bits >> shift)
    return (1 - 2 * (bits & 1)).astype(jnp.float32).astype(jnp.bfloat16)


def device_at(position):
    last = len(EXCHANGE_BITS) - 1
    return sum(((position >> (last - at)) & 1) << bit for at, bit in enumerate(EXCHANGE_BITS))


def position_of(device):
    last = len(EXCHANGE_BITS) - 1
    return sum(((device >> bit) & 1) << (last - at) for at, bit in enumerate(EXCHANGE_BITS))


def block_factor(exponents):
    factor = jnp.zeros(exponents.shape, jnp.float32)
    for exponent in range(low_power, high_power + 1):
        factor = jnp.where(exponents == exponent, jnp.float32(2.0 ** (-exponent)), factor)
    return factor


def butterfly(parts):
    parts = list(parts)
    step = 1
    while step < len(parts):
        for start in range(0, len(parts), 2 * step):
            for at in range(start, start + step):
                first, second = parts[at], parts[at + step]
                parts[at], parts[at + step] = first + second, first - second
        step *= 2
    return parts


def before_kernel(weights_ref, out_ref, held_ref, arrived):
    devices, _, cols = out_ref.shape
    pieces = arrived.shape[0]
    blocks = devices // pieces

    def fetch(piece):
        lanes = pl.ds(pl.multiple_of(piece * blocks * cols, blocks * cols), blocks * cols)
        return pltpu.make_async_copy(weights_ref.at[:, lanes], held_ref.at[:, lanes], arrived.at[piece])

    for piece in range(pieces):
        fetch(piece).start()

    def work(piece, carry):
        fetch(piece).wait()
        first = position_of(piece * blocks)
        for at in range(blocks):
            block = first + position_of(at)
            lanes = pl.ds(pl.multiple_of((piece * blocks + at) * cols, cols), cols)
            rows = [held_ref[LOW * k : LOW * (k + 1), lanes].astype(jnp.float32) for k in range(HIGH)]
            for k, row in enumerate(butterfly(rows)):
                out_ref[block, LOW * k : LOW * (k + 1), :] = row.astype(jnp.bfloat16)
        return carry

    lax.fori_loop(0, pieces, work, 0)


def before(weights, devices):
    rows, total = weights.shape
    return pl.pallas_call(
        before_kernel,
        out_shape=pltpu.VMEM((devices, rows, total // devices), jnp.bfloat16),
        in_specs=[pl.BlockSpec(memory_space=pl.ANY)],
        out_specs=pl.BlockSpec(memory_space=pltpu.VMEM),
        scratch_shapes=[pltpu.VMEM(weights.shape, jnp.bfloat16), pltpu.SemaphoreType.DMA((PIECES,))],
        compiler_params=pltpu.CompilerParams(vmem_limit_bytes=VMEM_BYTES),
    )(pltpu.with_memory_space_constraint(weights, pltpu.HBM))


def after_kernel(exponents_ref, received_ref, out_ref, peak_ref, factor_ref, stage_ref, even_ref, odd_ref, written):
    cols = received_ref.shape[-1]
    groups = INNER // LOW
    table = sylvester(LOW * LOW)
    scale = block_factor(exponents_ref[...]) * jnp.float32(1.0 / INNER)
    for half in range(scale.shape[0]):
        spread = jnp.broadcast_to(scale[half : half + 1, :], (INNER, OUTER))
        factor_ref[:, half * INNER : (half + 1) * INNER] = jnp.transpose(spread)

    def write(group, first):
        outer = slice(first * LOW, (first + WRITTEN) * LOW)
        rows = slice(group * LOW, (group + 1) * LOW)
        return pltpu.make_async_copy(
            stage_ref.at[group, outer], out_ref.at[outer, rows, :], written.at[group, first // WRITTEN]
        )

    def prepare(group, low, middle_ref):
        rows = slice(group * LOW, (group + 1) * LOW)
        parts = [received_ref[position_of(h * LOW + low), rows, :] for h in range(HIGH)]
        for h, part in enumerate(butterfly(parts)):
            lanes = slice(h % WIDE * cols, (h % WIDE + 1) * cols)
            middle_ref[h // WIDE, LOW * low : LOW * (low + 1), lanes] = part

    refs = (even_ref, odd_ref)
    for low in range(LOW):
        prepare(0, low, even_ref)
    largest = jnp.zeros((LOW, cols), jnp.bfloat16)
    for group in range(groups):
        for first in range(0, HIGH, WIDE):
            product = jnp.dot(table, refs[group % 2][first // WIDE], preferred_element_type=jnp.float32)
            if group + 1 < groups:
                for low in range(first * LOW // HIGH, (first + WIDE) * LOW // HIGH):
                    prepare(group + 1, low, refs[(group + 1) % 2])
            for low in range(LOW):
                for h in range(first, first + WIDE):
                    p = h * LOW + low
                    part = product[LOW * low : LOW * (low + 1), (h - first) * cols : (h - first + 1) * cols]
                    part = (part * factor_ref[p : p + 1, :]).astype(jnp.bfloat16)
                    largest = jnp.maximum(largest, jnp.abs(part))
                    stage_ref[group, p] = part
            if (first + WIDE) % WRITTEN == 0:
                write(group, first + WIDE - WRITTEN).start()

    peak = jnp.max(largest.astype(jnp.float32), axis=(0, 1), keepdims=True)
    peak_ref[...] = jnp.broadcast_to(peak.reshape(1, 1, 1), peak_ref.shape)
    for group in range(groups):
        for first in range(0, HIGH, WRITTEN):
            write(group, first).wait()


def after(exponents, received, devices):
    outer, inner, cols = received.shape
    groups = inner // LOW
    return pl.pallas_call(
        after_kernel,
        out_shape=(
            jax.ShapeDtypeStruct((outer, inner, cols), jnp.bfloat16),
            pltpu.VMEM((devices, 1, 128), jnp.float32),
        ),
        in_specs=[pl.BlockSpec(memory_space=pltpu.VMEM)] * 2,
        out_specs=(pl.BlockSpec(memory_space=pl.ANY), pl.BlockSpec(memory_space=pltpu.VMEM)),
        scratch_shapes=[
            pltpu.VMEM((outer, cols), jnp.float32),
            pltpu.VMEM((groups, outer, LOW, cols), jnp.bfloat16),
            pltpu.VMEM((HIGH // WIDE, LOW * LOW, WIDE * cols), jnp.bfloat16),
            pltpu.VMEM((HIGH // WIDE, LOW * LOW, WIDE * cols), jnp.bfloat16),
            pltpu.SemaphoreType.DMA((groups, HIGH // WRITTEN)),
        ],
        compiler_params=pltpu.CompilerParams(vmem_limit_bytes=VMEM_BYTES),
    )(exponents, pltpu.with_memory_space_constraint(received, pltpu.VMEM))


def on_device(weights, exponents):
    axes = ("fsdp", "rep")
    devices = lax.axis_size("fsdp") * lax.axis_size("rep")
    cols = weights.shape[1] // devices
    packed = before(weights, devices)
    order = [[device_at(position) for position in range(devices)]]
    exchange = functools.partial(
        lax.all_to_all, axis_name=axes, split_axis=0, concat_axis=0, axis_index_groups=order, tiled=True
    )
    received = exchange(packed)
    quantized, peaks = after(exponents.T, received, devices)
    shared = exchange(peaks)
    return (quantized.reshape(OUTER * INNER, cols), jnp.max(shared.reshape(devices, 128)[:, :1]))


def solution(mesh):
    return jax.shard_map(
        on_device,
        mesh=mesh,
        in_specs=(P(("fsdp", "rep"), None), P(None, ("fsdp", "rep"))),
        out_specs=(P(None, ("fsdp", "rep")), P()),
        check_vma=False,
    )
```
